256 devices in a mesh: dp: 16 (over z_hi, y, core), tensor: 16 (over z_lo, x).
Axes of the slice: x: 4, y: 4, z: 8 (z_hi: 2, z_lo: 4; z = z_hi * 4 + z_lo), core: 2. Of those that a mesh axis runs over, the one named last changes fastest.
Arguments:
- layer_input: bfloat16 [12288, 8192], P('dp', 'tensor'), may hold values from -6 to 6
- gate_saved: bfloat16 [12288, 14336], P('dp', 'tensor'), may hold values from -6 to 6
- up_saved: bfloat16 [12288, 14336], P('dp', 'tensor'), may hold values from -6 to 6
- grad_out: bfloat16 [12288, 8192], P('dp', 'tensor'), may hold values from -6 to 6
- down_weight: bfloat16 [14336, 8192], P('tensor', 'dp'), may hold values from -0.046875 to 0.046875
- hidden_proj: bfloat16 [14336, 64], P('tensor'), may hold values from -0.046875 to 0.046875
- model_proj: bfloat16 [8192, 64], P('tensor'), may hold values from -0.0625 to 0.0625
- query_sketch: bfloat16 [4096, 8192], P('dp', 'tensor'), may hold values from -6 to 6
- resp_lengths: int32 [96, 2], P('dp'), may hold values from 16 to 64
- chosen_index: int32 [96], P('dp'), may hold values from 0 to 1
Outputs:
- sketch: float32 [96, 8192], P('dp', 'tensor')
- scores: float32 [96, 4096], P('tensor', 'dp')
The draws below stay inside these ranges and needn't reach their ends.
All inputs are finite; a program needn't handle non-finite values.
Results may differ from the reference program's by a relative error of at most 0.0095.
Values may be sent and summed in bfloat16 or wider, within the bound.
No kernel may reach another device: no remote copies, remote signals or barrier semaphores. Data moves between devices by JAX's collectives and lax.ppermute only.
A program may use at most 128 MiB of HBM per device.

```python
import jax
import jax.numpy as jnp
from jax import lax

D = 8192
FF = 14336
SK = 64
RESP = 64
QUERIES = 4096
PAIRS = 96
TOKENS = 12288
ENTRIES = 8192


def place_ends(result, rng, smallest, largest):
    longest = result.shape.index(max(result.shape))
    spots = []
    for shift in (0, 1):
        where = [jax.random.randint(jax.random.fold_in(rng, axis), (), 0, length) for axis, length in enumerate(result.shape)]
        where[longest] = (where[longest] + shift) % result.shape[longest]
        spots.append(tuple(where))
    return result.at[spots[0]].set(smallest).at[spots[1]].set(largest)


def shard_levels(key, extent, split, smallest, top_value):
    gain = 1.0
    for position, shards_of in split:
        draws = jax.random.uniform(jax.random.fold_in(jax.random.fold_in(key, 6), position), (shards_of,), jnp.float32, smallest / len(split), top_value / len(split))
        gain = gain * jnp.repeat(jnp.exp(draws), extent[position] // shards_of).reshape((-1,) + (1,) * (len(extent) - 1 - position))
    return gain


def noise(rng, shape, width, bound, shards=(), held_as=jnp.bfloat16):
    entries = width * jax.random.normal(rng, shape, jnp.float32)
    if shards:
        entries = entries * shard_levels(rng, shape, shards, -0.22, 0.18)
    return jnp.clip(entries, -bound, bound).astype(held_as)


def setup_inputs(seed: int = 0) -> dict:
    seeds = jax.random.split(jax.random.key(seed), 11)
    return {
        "layer_input": noise(seeds[0], (TOKENS, D), 1.0, 6.0, ((0, 16), (1, 16))),
        "gate_saved": noise(seeds[1], (TOKENS, FF), 1.0, 6.0, ((0, 16), (1, 16))),
        "up_saved": noise(seeds[2], (TOKENS, FF), 1.0, 6.0, ((0, 16), (1, 16))),
        "grad_out": noise(seeds[3], (TOKENS, D), 1.0, 6.0, ((0, 16), (1, 16))),
        "down_weight": noise(seeds[4], (FF, D), FF ** -0.5, 0.046875, ((0, 16), (1, 16))),
        "hidden_proj": noise(seeds[5], (FF, SK), FF ** -0.5, 0.046875, ((0, 16),)),
        "model_proj": noise(seeds[6], (D, SK), D ** -0.5, 0.0625, ((0, 16),)),
        "query_sketch": noise(seeds[7], (QUERIES, ENTRIES), 1.0, 6.0, ((0, 16), (1, 16))),
        "resp_lengths": place_ends(jax.random.randint(seeds[8], (PAIRS, 2), RESP // 4, RESP + 1), jax.random.fold_in(seeds[8], 1), RESP // 4, RESP).astype(jnp.int32),
        "chosen_index": place_ends(jax.random.randint(seeds[9], (PAIRS,), 0, 2), jax.random.fold_in(seeds[9], 1), 0, 1).astype(jnp.int32),
    }


sketch_scale = 0.25

def reference(layer_input, gate_saved, up_saved, grad_out, down_weight, hidden_proj, model_proj, query_sketch, resp_lengths, chosen_index):
    span = 2 * RESP
    slots = jnp.arange(RESP, dtype=jnp.int32)
    sides = jnp.arange(2, dtype=jnp.int32)
    live = slots[None, None, :] < resp_lengths[:, :, None]
    signs = jnp.where(sides[None, :] == chosen_index[:, None], 1.0, -1.0).astype(jnp.float32)
    weight = jnp.where(live, signs[:, :, None], 0.0).astype(jnp.float32).reshape(PAIRS, span)
    proj_wide = hidden_proj.astype(jnp.float32)

    def one_pair(block):
        inputs, gates, ups, grads, weights = block
        backward = jnp.dot(grads, down_weight.T, preferred_element_type=jnp.float32)
        gate32 = gates.astype(jnp.float32)
        up32 = ups.astype(jnp.float32)
        sig = jax.nn.sigmoid(gate32)
        hidden = (gate32 * sig * up32).astype(jnp.bfloat16)
        dgate = backward * up32 * sig * (1.0 + gate32 * (1.0 - sig))
        left_down = jnp.dot(hidden, hidden_proj, preferred_element_type=jnp.float32)
        right_down = jnp.dot(grads, model_proj, preferred_element_type=jnp.float32)
        left_gate = jnp.dot(inputs, model_proj, preferred_element_type=jnp.float32)
        right_gate = jnp.dot(dgate, proj_wide, precision=lax.Precision.HIGHEST, preferred_element_type=jnp.float32)
        down = jnp.einsum('t,tk,tl->kl', weights, left_down, right_down) * sketch_scale
        gatesk = jnp.einsum('t,tk,tl->kl', weights, left_gate, right_gate) * sketch_scale
        return jnp.concatenate([down.reshape(SK * SK), gatesk.reshape(SK * SK)])
    blocks = (layer_input.reshape(PAIRS, span, D), gate_saved.reshape(PAIRS, span, FF), up_saved.reshape(PAIRS, span, FF), grad_out.reshape(PAIRS, span, D), weight)
    sketch = lax.map(one_pair, blocks)
    scores = jnp.dot(sketch, query_sketch.astype(jnp.float32).T, precision=lax.Precision.HIGHEST, preferred_element_type=jnp.float32) / jnp.sqrt(jnp.float32(2 * SK * SK))
    return (sketch, scores)
```

```python
import jax
import jax.numpy as jnp
from jax import lax
from jax.experimental import pallas as pl
from jax.experimental.pallas import tpu as pltpu
from jax.sharding import PartitionSpec as P

SCALE = 0.25
AXES = ("dp", "tensor")
F32 = jnp.float32
BF16 = jnp.bfloat16
TRANSPOSED = (((1,), (1,)), ((), ()))


def flat(x, y, z, c):
    return (((z // 4) * 4 + y) * 2 + c) * 16 + (z % 4) * 4 + x


def move(value, where):
    pairs = []
    for z in range(8):
        for y in range(4):
            for x in range(4):
                for c in range(2):
                    nx, ny, nz, nc = where(x, y, z, c)
                    pairs.append((flat(x, y, z, c), flat(nx % 4, ny % 4, nz % 8, nc % 2)))
    return lax.ppermute(value, AXES, pairs)


def side(c):
    return 1 - 2 * c


def ring_x(sign):
    return lambda x, y, z, c: (x + sign * side(c), y, z, c)


def ring_y(sign):
    return lambda x, y, z, c: (x, y + sign * side(c), z, c)


def shift_x(step):
    return lambda x, y, z, c: (x + step, y, z, c)


def shift_y(step):
    return lambda x, y, z, c: (x, y + step, z, c)


def line_z(step):
    return lambda x, y, z, c: (x, y, (z // 4) * 4 + (z + step) % 4, c)


def line_z_both(x, y, z, c):
    return line_z(side(c))(x, y, z, c)


def swap_core(x, y, z, c):
    return (x, y, z, c + 1)


def swap_half(x, y, z, c):
    return (x, y, z + 4, c)


def after(value, *others):
    return lax.optimization_barrier((value,) + others)[0]


class Chain:
    def __init__(self, depth):
        self.depth = depth
        self.done = []

    def move(self, value, where, *others):
        waits = list(others)
        if len(self.done) >= self.depth:
            waits.append(self.done[-self.depth])
        if waits:
            value = after(value, *waits)
        out = move(value, where)
        self.done.append(out)
        return out


def pick(buffer, index, axis):
    return lax.dynamic_index_in_dim(buffer, index, axis, keepdims=False)


def put(buffer, value, index):
    return lax.dynamic_update_index_in_dim(buffer, value, index, 0)


def grouped(count, first, last, index_ref, *refs):
    pieces = refs[:count]
    weight_ref = refs[count]
    rest = list(refs[count + 1 :])
    step = pl.program_id(0)
    start_ref = None if first else rest.pop(0)
    if last:
        slope_ref, proj_ref, left_ref, down_ref, out_ref, sum_ref = rest
    else:
        (sum_ref,) = rest
    for n in range(count):

        @pl.when(step == n)
        def _(n=n):
            product = lax.dot_general(
                pieces[n][...], weight_ref[0], TRANSPOSED, preferred_element_type=F32
            )
            if n > 0:
                sum_ref[...] += product
            elif first:
                sum_ref[...] = product
            else:
                sum_ref[...] = start_ref[...] + product

    if last:

        @pl.when(step == count - 1)
        def _():
            pairs = down_ref.shape[0]
            span = left_ref.shape[0] // pairs
            for p in range(pairs):
                rows = pl.ds(p * span, span)
                dgate = (sum_ref[rows, :] * slope_ref[rows, :].astype(F32)).astype(BF16)
                e = jnp.dot(dgate, proj_ref[...], preferred_element_type=F32)
                gates = lax.dot_general(
                    left_ref[rows, :],
                    e,
                    (((0,), (0,)), ((), ())),
                    precision=lax.Precision.HIGHEST,
                    preferred_element_type=F32,
                )
                total = down_ref[p] + gates
                out_ref[:, p] = total.reshape(8, 8, 128)


def product_step(pieces, weights, index, start, tail=None):
    count = len(pieces)
    rows, depth = pieces[0].shape
    units = weights.shape[1]
    first, last = start is None, tail is not None

    def whole(shape):
        return pl.BlockSpec(shape, lambda n, k: (0,) * len(shape))

    in_specs = [whole(p.shape) for p in pieces]
    in_specs.append(pl.BlockSpec((1, units, depth), lambda n, k: (k[n], 0, 0)))
    args = list(pieces) + [weights]
    if not first:
        in_specs.append(whole(start.shape))
        args.append(start)
    scratch = []
    if last:
        for t in tail:
            in_specs.append(whole(t.shape))
            args.append(t)
        pairs = tail[3].shape[0]
        out_shape = jax.ShapeDtypeStruct((8, pairs, 8, 128), F32)
        scratch = [pltpu.VMEM((rows, units), F32)]
    else:
        out_shape = jax.ShapeDtypeStruct((rows, units), F32)
    return pl.pallas_call(
        lambda *refs: grouped(count, first, last, *refs),
        out_shape=out_shape,
        grid_spec=pltpu.PrefetchScalarGridSpec(
            num_scalar_prefetch=1,
            grid=(count,),
            in_specs=in_specs,
            out_specs=whole(out_shape.shape),
            scratch_shapes=scratch,
        ),
        compiler_params=pltpu.CompilerParams(vmem_limit_bytes=40 * 2**20),
        cost_estimate=pl.CostEstimate(
            flops=2 * count * rows * units * depth,
            bytes_accessed=count * (rows + units) * depth * 2 + 8 * rows * units,
            transcendentals=0,
        ),
    )(jnp.stack(index).astype(jnp.int32), *args)


def scatter_sum(parts, zl, x):
    planes = parts.shape[0]
    total = pick(parts, x, 1)
    for step in (1, 2, 3):
        total = total + move(pick(parts, (x + step) % 4, 1), shift_x(step))
    out = pick(total, zl % planes, 0)
    for step in (1, 2, 3):
        out = out + move(pick(total, (zl + step) % planes, 0), line_z(step))
    return out


def gather_pairs(value, zh, y, c):
    halves = jnp.zeros((2,) + value.shape, value.dtype)
    halves = put(halves, value, zh)
    halves = put(halves, move(value, swap_half), 1 - zh)
    rows = jnp.zeros((4,) + halves.shape, value.dtype)
    rows = put(rows, halves, y)
    for step in (1, 2, 3):
        rows = put(rows, move(halves, shift_y(step)), (y - step) % 4)
    every = jnp.zeros((2,) + rows.shape, value.dtype)
    every = put(every, rows, c)
    every = put(every, move(rows, swap_core), 1 - c)
    return every


def local(
    layer_input,
    gate_saved,
    up_saved,
    grad_out,
    down_weight,
    hidden_proj,
    model_proj,
    query_sketch,
    resp_lengths,
    chosen_index,
):
    tok_rows = grad_out.shape[0]
    pairs = resp_lengths.shape[0]
    span = tok_rows // pairs
    half = span // 2
    sk = hidden_proj.shape[1]
    entries = 2 * sk * sk
    i = lax.axis_index("dp")
    j = lax.axis_index("tensor")
    zh, y, c = i // 8, (i // 2) % 4, i % 2
    zl, x = j // 4, j % 4
    sign = 1 - 2 * c
    around = (0, -sign, sign, 2)

    chain_x, chain_y, chain_z = Chain(2), Chain(1), Chain(1)
    chain_core, chain_sum = Chain(1), Chain(1)

    blocks = [grad_out]
    pieces = []
    for hop in range(4):
        block = blocks[hop]
        if hop < 3:
            blocks.append(chain_z.move(block, line_z_both))
        ahead = chain_x.move(block, ring_x(1))
        behind = chain_x.move(block, ring_x(-1))
        across = chain_x.move(ahead, ring_x(1))
        pieces.append([block, ahead, behind, across])
    far = move(down_weight, swap_half)
    wbuf = jnp.zeros((16,) + down_weight.shape, BF16)
    for part, where in ((down_weight, zh), (far, 1 - zh)):
        ahead = chain_y.move(part, ring_y(1))
        behind = chain_y.move(part, ring_y(-1))
        across = chain_y.move(ahead, ring_y(1))
        for value, step in zip((part, ahead, behind, across), around):
            mine = (where * 4 + (y + step) % 4) * 2 + c
            other = (where * 4 + (y - step) % 4) * 2 + 1 - c
            wbuf = put(wbuf, value, mine)
            wbuf = put(wbuf, chain_core.move(value, swap_core), other)

    terms = jnp.concatenate(
        [
            jnp.dot(grad_out, model_proj, preferred_element_type=F32),
            jnp.dot(layer_input, model_proj, preferred_element_type=F32),
        ],
        axis=1,
    )
    quarters = terms.reshape(4, tok_rows // 4, 2 * sk)
    mine = pick(quarters, x, 0)
    for step in (1, 2, 3):
        mine = mine + chain_sum.move(pick(quarters, (x + step) % 4, 0), shift_x(step), blocks[1])
    total = mine
    for step in (1, 2, 3):
        total = total + chain_sum.move(mine, line_z(step))
    full = jnp.zeros_like(quarters)
    full = put(full, total, x)
    for step in (1, 2, 3):
        full = put(full, chain_sum.move(total, shift_x(step)), (x - step) % 4)
    full = full.reshape(tok_rows, 2 * sk)

    slots = jnp.arange(half, dtype=jnp.int32)
    sides = jnp.arange(2, dtype=jnp.int32)
    live = slots[None, None, :] < resp_lengths[:, :, None]
    signs = jnp.where(sides[None, :] == chosen_index[:, None], SCALE, -SCALE).astype(F32)
    weight = jnp.where(live, signs[:, :, None], 0.0).reshape(tok_rows, 1)

    gate32 = gate_saved.astype(F32)
    up32 = up_saved.astype(F32)
    sig = jax.nn.sigmoid(gate32)
    hidden = (gate32 * sig * up32).astype(BF16)
    slope = (up32 * sig * (1.0 + gate32 * (1.0 - sig))).astype(BF16)
    a = jnp.dot(hidden, hidden_proj, preferred_element_type=F32)

    down = jnp.einsum(
        "ptk,ptl->pkl",
        (a * weight).reshape(pairs, span, sk),
        full[:, :sk].reshape(pairs, span, sk),
        precision=lax.Precision.HIGH,
    )
    down = jnp.pad(down, ((0, 0), (0, 0), (0, sk)))
    left = full[:, sk:] * weight
    proj = jnp.pad(hidden_proj, ((0, 0), (sk, 0)))

    backward = None
    for hop in range(4):
        from_zl = (zl - hop * sign) % 4
        index = [from_zl * 4 + (x + step) % 4 for step in around]
        if hop < 3:
            backward = product_step(pieces[hop], wbuf, index, backward)
        else:
            backward = product_step(pieces[hop][:3], wbuf, index[:3], backward)
            parts = product_step(
                pieces[hop][3:], wbuf, index[3:], backward, (slope, proj, left, down)
            )

    both = scatter_sum(parts.reshape(2, 4, pairs, 8, 2 * sk), zl, x)
    mine = jnp.where(zl >= 2, both[:, :, sk:], both[:, :, :sk])
    sketch = mine.reshape(pairs, 8 * sk)
    every = gather_pairs(sketch, zh, y, c)
    partial = lax.dot_general(
        every.reshape(16 * pairs, 8 * sk),
        query_sketch.astype(F32),
        TRANSPOSED,
        precision=lax.Precision.HIGHEST,
        preferred_element_type=F32,
    ) / jnp.sqrt(F32(entries))
    partial = partial.reshape(2, 4, 2, pairs, -1).transpose(2, 1, 0, 3, 4)
    scores = scatter_sum(partial.reshape(4, 4, pairs, -1), zl, x)
    return (sketch, scores)


def solution(mesh):
    return jax.shard_map(
        local,
        mesh=mesh,
        in_specs=(
            P("dp", "tensor"),
            P("dp", "tensor"),
            P("dp", "tensor"),
            P("dp", "tensor"),
            P("tensor", "dp"),
            P("tensor", None),
            P("tensor", None),
            P("dp", "tensor"),
            P("dp", None),
            P("dp"),
        ),
        out_specs=(P("dp", "tensor"), P("tensor", "dp")),
        check_vma=False,
    )
```

```python
import jax
import jax.numpy as jnp
from jax import lax
from jax.experimental import pallas as pl
from jax.experimental.pallas import tpu as pltpu
from jax.sharding import PartitionSpec as P

SCALE = 0.25
AXES = ("dp", "tensor")
F32 = jnp.float32
BF16 = jnp.bfloat16
TRANSPOSED = (((1,), (1,)), ((), ()))


def flat(x, y, z, c):
    return (((z // 4) * 4 + y) * 2 + c) * 16 + (z % 4) * 4 + x


def move(value, where):
    pairs = []
    for z in range(8):
        for y in range(4):
            for x in range(4):
                for c in range(2):
                    nx, ny, nz, nc = where(x, y, z, c)
                    pairs.append((flat(x, y, z, c), flat(nx % 4, ny % 4, nz % 8, nc % 2)))
    return lax.ppermute(value, AXES, pairs)


def side(c):
    return 1 - 2 * c


def ring_x(sign):
    return lambda x, y, z, c: (x + sign * side(c), y, z, c)


def ring_y(sign):
    return lambda x, y, z, c: (x, y + sign * side(c), z, c)


def shift_x(step):
    return lambda x, y, z, c: (x + step, y, z, c)


def shift_y(step):
    return lambda x, y, z, c: (x, y + step, z, c)


def line_z(step):
    return lambda x, y, z, c: (x, y, (z // 4) * 4 + (z + step) % 4, c)


def line_z_both(x, y, z, c):
    return line_z(side(c))(x, y, z, c)


def swap_core(x, y, z, c):
    return (x, y, z, c + 1)


def swap_half(x, y, z, c):
    return (x, y, z + 4, c)


def pick(buffer, index, axis):
    return lax.dynamic_index_in_dim(buffer, index, axis, keepdims=False)


def put(buffer, value, index):
    return lax.dynamic_update_index_in_dim(buffer, value, index, 0)


SLOTS = 4


def product_kernel(count, last, index_ref, *refs):
    pieces, refs = refs[:count], refs[count:]
    near_own, near_other, far_own, far_other, refs = refs[0], refs[1], refs[2:4], refs[4:6], refs[6:]
    early = []
    if last:
        start_hbm, slope_hbm, proj_ref, left_ref, down_ref = refs[:5]
        out_refs, refs = refs[5:9], refs[9:]
        left_buf, right_buf, left_sem, right_sem, sum_ref, start_ref, slope_ref, tail_sem = refs
        early = [
            pltpu.make_async_copy(start_hbm, start_ref, tail_sem.at[0]),
            pltpu.make_async_copy(slope_hbm, slope_ref, tail_sem.at[1]),
        ]
    else:
        sum_ref, left_buf, right_buf, left_sem, right_sem = refs
    half = sum_ref.shape[1] // 2

    def copies(n):
        slot = n % SLOTS
        one = pltpu.make_async_copy(pieces[n], left_buf.at[slot], left_sem.at[slot])
        one.start()
        waits = [one]
        place = index_ref[n]
        for part in range(2):
            rows = pl.ds(part * half, half)
            target = right_buf.at[slot, rows]
            sem = right_sem.at[slot, part]
            for which, source in enumerate(
                (
                    near_own.at[place % 4, rows],
                    near_other.at[place % 4, rows],
                    far_own[part].at[place % 4],
                    far_other[part].at[place % 4],
                )
            ):

                @pl.when(place // 4 == which)
                def _(source=source):
                    pltpu.make_async_copy(source, target, sem).start()

            waits.append(pltpu.make_async_copy(near_own.at[0, rows], target, sem))
        return waits

    ahead = SLOTS - 1
    waits = [copies(n) for n in range(min(ahead, count))]
    for n in range(count):
        if n + ahead < count:
            waits.append(copies(n + ahead))
        elif n + ahead == count:
            for copy in early:
                copy.start()
        for wait in waits[n]:
            wait.wait()
        product = lax.dot_general(
            left_buf[n % SLOTS], right_buf[n % SLOTS], TRANSPOSED, preferred_element_type=F32
        )
        if n:
            sum_ref[...] += product
        else:
            sum_ref[...] = product

    if last:
        column = index_ref[count]
        for copy in early:
            copy.wait()
        pairs = down_ref.shape[0]
        span = left_ref.shape[0] // pairs
        for p in range(pairs):
            here = pl.ds(p * span, span)
            if p % 2 == 0:
                two = pl.ds(p * span, 2 * span)
                total = (sum_ref[two, :] + start_ref[two, :]) * slope_ref[two, :].astype(F32)
                e = jnp.dot(total.astype(BF16), proj_ref[...], preferred_element_type=F32)
                e = e.astype(BF16)
            gates = lax.dot_general(
                left_ref[here, :],
                e[(p % 2) * span : (p % 2 + 1) * span],
                (((0,), (0,)), ((), ())),
                preferred_element_type=F32,
            )
            total = (down_ref[p] + gates).reshape(2, 4, 8, 128)
            for m in range(4):
                for away in range(4):

                    @pl.when((column + away) % 4 == m)
                    def _(m=m, away=away, total=total):
                        out_refs[away][:, p] = total[:, m]


ANYWHERE = pl.BlockSpec(memory_space=pl.ANY)
IN_VMEM = pl.BlockSpec(memory_space=pltpu.VMEM)
IN_SMEM = pl.BlockSpec(memory_space=pltpu.SMEM)


def products(pieces, weights, index, tail=()):
    count = len(pieces)
    rows, depth = pieces[0].shape
    units = weights[0].shape[1]
    last = bool(tail)
    scratch = [
        pltpu.VMEM((SLOTS, rows, depth), BF16),
        pltpu.VMEM((SLOTS, units, depth), BF16),
        pltpu.SemaphoreType.DMA((SLOTS,)),
        pltpu.SemaphoreType.DMA((SLOTS, 2)),
    ]
    out_shape = jax.ShapeDtypeStruct((rows, units), F32)
    out_specs = IN_VMEM
    if last:
        scratch += [
            pltpu.VMEM((rows, units), F32),
            pltpu.VMEM((rows, units), F32),
            pltpu.VMEM((rows, units), BF16),
            pltpu.SemaphoreType.DMA((2,)),
        ]
        out_shape = [jax.ShapeDtypeStruct((2, tail[4].shape[0], 8, 128), F32)] * 4
        out_specs = [IN_VMEM] * 4
    return pl.pallas_call(
        lambda *refs: product_kernel(count, last, *refs),
        out_shape=out_shape,
        in_specs=[IN_SMEM]
        + [ANYWHERE] * (count + len(weights) + min(len(tail), 2))
        + [IN_VMEM] * max(len(tail) - 2, 0),
        out_specs=out_specs,
        scratch_shapes=scratch,
        compiler_params=pltpu.CompilerParams(vmem_limit_bytes=58 * 2**20),
        cost_estimate=pl.CostEstimate(
            flops=2 * count * rows * units * depth,
            bytes_accessed=2 * count * (rows + units) * depth + 4 * rows * units,
            transcendentals=0,
        ),
    )(index, *pieces, *weights, *tail)


def sum_columns(slabs):
    total = slabs[0]
    for step in (1, 2, 3):
        total = total + move(slabs[step], shift_x(step))
    return total


def gather_pairs(value, zh, y, c):
    halves = jnp.zeros((2,) + value.shape, value.dtype)
    halves = put(halves, value, zh)
    halves = put(halves, move(value, swap_half), 1 - zh)
    rows = jnp.zeros((4,) + halves.shape, value.dtype)
    rows = put(rows, halves, y)
    for step in (1, 2, 3):
        rows = put(rows, move(halves, shift_y(step)), (y - step) % 4)
    every = jnp.zeros((2,) + rows.shape, value.dtype)
    every = put(every, rows, c)
    every = put(every, move(rows, swap_core), 1 - c)
    return every


def local(
    layer_input,
    gate_saved,
    up_saved,
    grad_out,
    down_weight,
    hidden_proj,
    model_proj,
    query_sketch,
    resp_lengths,
    chosen_index,
):
    tok_rows = grad_out.shape[0]
    pairs = resp_lengths.shape[0]
    span = tok_rows // pairs
    half = span // 2
    sk = hidden_proj.shape[1]
    entries = 2 * sk * sk
    i = lax.axis_index("dp")
    j = lax.axis_index("tensor")
    zh, y, c = i // 8, (i // 2) % 4, i % 2
    zl, x = j // 4, j % 4
    sign = 1 - 2 * c

    def turn(*values):
        return lax.optimization_barrier(values)

    def along_y(value):
        groups = [[(h * 4 + r) * 2 + k for r in range(4)] for h in range(2) for k in range(2)]
        return lax.all_gather(value, "dp", axis=0, tiled=False, axis_index_groups=groups)

    sixteenth = tok_rows // 16
    mid = down_weight.shape[0] // 2
    near_own = along_y(down_weight)

    terms = jnp.concatenate(
        [
            jnp.dot(grad_out, model_proj, preferred_element_type=F32),
            jnp.dot(layer_input, model_proj, preferred_element_type=F32),
        ],
        axis=1,
    ).astype(BF16)
    dealt = lax.all_to_all(terms, "tensor", 0, 0, tiled=True)
    ahead0 = move(grad_out, ring_x(1))
    behind0 = move(grad_out, ring_x(-1))
    across0 = move(grad_out, shift_x(2))
    hop1 = move(grad_out, line_z_both)
    far_a = move(down_weight[:mid], swap_half)
    ahead0, behind0, across0, hop1, far_a, weight_rows, dealt, near_own = turn(
        ahead0, behind0, across0, hop1, far_a, down_weight, dealt, near_own
    )

    far_own_a = along_y(far_a)
    mine = dealt.reshape(16, sixteenth, 2 * sk).astype(F32).sum(axis=0).astype(BF16)
    ahead1 = move(hop1, ring_x(1))
    behind1 = move(hop1, ring_x(-1))
    across1 = move(hop1, shift_x(2))
    hop2 = move(hop1, line_z_both)
    far_b = move(weight_rows[mid:], swap_half)
    ahead1, behind1, across1, hop2, far_b, far_own_a, mine, gate_saved = turn(
        ahead1, behind1, across1, hop2, far_b, far_own_a, mine, gate_saved
    )

    far_own_b = along_y(far_b)
    full = lax.all_to_all(
        jnp.broadcast_to(mine, (16, sixteenth, 2 * sk)).reshape(tok_rows, 2 * sk),
        "tensor", 0, 0, tiled=True,
    )
    gate32 = gate_saved.astype(F32)
    up32 = up_saved.astype(F32)
    sig = jax.nn.sigmoid(gate32)
    hidden = (gate32 * sig * up32).astype(BF16)
    slope = (up32 * sig * (1.0 + gate32 * (1.0 - sig))).astype(BF16)
    a = jnp.dot(hidden, hidden_proj, preferred_element_type=F32)
    ahead2 = move(hop2, ring_x(1))
    behind2 = move(hop2, ring_x(-1))
    across2 = move(hop2, shift_x(2))
    hop3 = move(hop2, line_z_both)
    near_other = move(near_own, swap_core)
    ahead2, behind2, across2, hop3, near_other, full, slope, a, far_own_b = turn(
        ahead2, behind2, across2, hop3, near_other, full, slope, a, far_own_b
    )
    full = full.astype(F32)

    ahead3 = move(hop3, ring_x(1))
    behind3 = move(hop3, ring_x(-1))
    across3 = move(across2, line_z_both)
    far_other_b = move(far_own_b, swap_core)
    far_other_a = move(far_own_a, swap_core)
    pieces = [
        grad_out, ahead0, behind0, across0,
        hop1, ahead1, behind1, across1,
        hop2, ahead2, behind2, across2,
        hop3, ahead3, behind3, across3,
    ]
    k = jnp.stack(
        [
            ((zl - hop * sign) % 4) * 4 + (x + away) % 4
            for hop in range(4)
            for away in (0, -sign, sign, 2)
        ]
    ).astype(jnp.int32)
    index = jnp.where(k // 8 == zh, 0, 8) + jnp.where(k % 2 == c, 0, 4) + (k // 2) % 4

    slots = jnp.arange(half, dtype=jnp.int32)
    sides = jnp.arange(2, dtype=jnp.int32)
    live = slots[None, None, :] < resp_lengths[:, :, None]
    signs = jnp.where(sides[None, :] == chosen_index[:, None], SCALE, -SCALE).astype(F32)
    weight = jnp.where(live, signs[:, :, None], 0.0).reshape(tok_rows, 1)

    down = jnp.einsum(
        "ptk,ptl->pkl",
        (a * weight).reshape(pairs, span, sk),
        full[:, :sk].reshape(pairs, span, sk),
        precision=lax.Precision.HIGH,
    )
    down = jnp.pad(down, ((0, 0), (0, 0), (0, sk)))
    left = (full[:, sk:] * weight).astype(BF16)
    proj = jnp.pad(hidden_proj, ((0, 0), (sk, 0)))

    weights = (near_own, near_other, far_own_a, far_own_b, far_other_a, far_other_b)
    first = products(pieces[:12], weights, index[:12])
    slabs = products(
        pieces[12:],
        weights,
        jnp.concatenate([index[12:], x.astype(jnp.int32)[None]]),
        (first, slope, proj, left, down),
    )

    both = sum_columns(slabs)
    line = zl % 2
    out = pick(both, line, 0)
    for step in (1, 2, 3):
        out = out + move(pick(both, (line + step) % 2, 0), line_z(step))
    mine = jnp.where(zl >= 2, out[:, :, sk:], out[:, :, :sk])
    sketch = mine.reshape(pairs, 8 * sk)
    every = gather_pairs(sketch, zh, y, c)
    partial = lax.dot_general(
        every.reshape(16 * pairs, 8 * sk),
        query_sketch.astype(F32),
        TRANSPOSED,
        precision=lax.Precision.HIGHEST,
        preferred_element_type=F32,
    ) / jnp.sqrt(F32(entries))
    partial = partial.reshape(2, 2, 2, 2, pairs, -1).transpose(2, 0, 3, 1, 4, 5)
    grid = partial.reshape(4, 4, pairs, -1)
    summed = sum_columns([pick(grid, (x + step) % 4, 0) for step in range(4)])
    scores = pick(summed, zl, 0)
    for step in (1, 2, 3):
        scores = scores + move(pick(summed, (zl + step) % 4, 0), line_z(step))
    return (sketch, scores)


def solution(mesh):
    return jax.shard_map(
        local,
        mesh=mesh,
        in_specs=(
            P("dp", "tensor"),
            P("dp", "tensor"),
            P("dp", "tensor"),
            P("dp", "tensor"),
            P("tensor", "dp"),
            P("tensor", None),
            P("tensor", None),
            P("dp", "tensor"),
            P("dp", None),
            P("dp"),
        ),
        out_specs=(P("dp", "tensor"), P("tensor", "dp")),
        check_vma=False,
    )
```

```python
import jax
import jax.numpy as jnp
from jax import lax
from jax.experimental import pallas as pl
from jax.experimental.pallas import tpu as pltpu
from jax.sharding import PartitionSpec as P

SCALE = 0.25
AXES = ("dp", "tensor")
F32 = jnp.float32
BF16 = jnp.bfloat16
TRANSPOSED = (((1,), (1,)), ((), ()))


def flat(x, y, z, c):
    return (((z // 4) * 4 + y) * 2 + c) * 16 + (z % 4) * 4 + x


def move(value, where):
    pairs = []
    for z in range(8):
        for y in range(4):
            for x in range(4):
                for c in range(2):
                    nx, ny, nz, nc = where(x, y, z, c)
                    pairs.append((flat(x, y, z, c), flat(nx % 4, ny % 4, nz % 8, nc % 2)))
    return lax.ppermute(value, AXES, pairs)


def side(c):
    return 1 - 2 * c


def ring_x(sign):
    return lambda x, y, z, c: (x + sign * side(c), y, z, c)


def ring_y(sign):
    return lambda x, y, z, c: (x, y + sign * side(c), z, c)


def shift_x(step):
    return lambda x, y, z, c: (x + step, y, z, c)


def shift_y(step):
    return lambda x, y, z, c: (x, y + step, z, c)


def line_z(step):
    return lambda x, y, z, c: (x, y, (z // 4) * 4 + (z + step) % 4, c)


def line_z_both(x, y, z, c):
    return line_z(side(c))(x, y, z, c)


def across_both(x, y, z, c):
    return shift_x(2)(x, y, z, c) if c == 0 else line_z_both(x, y, z, c)


def swap_core(x, y, z, c):
    return (x, y, z, c + 1)


def swap_half(x, y, z, c):
    return (x, y, z + 4, c)


def pick(buffer, index, axis):
    return lax.dynamic_index_in_dim(buffer, index, axis, keepdims=False)


def put(buffer, value, index):
    return lax.dynamic_update_index_in_dim(buffer, value, index, 0)


SLOTS = 4


def product_kernel(count, last, index_ref, *refs):
    pieces, refs = refs[:count], refs[count:]
    near_own, near_other, far_own, far_other, refs = refs[0], refs[1], refs[2:4], refs[4:6], refs[6:]
    early = []
    if last:
        start_hbm, slope_hbm, proj_ref, left_ref, down_ref = refs[:5]
        out_refs, refs = refs[5:9], refs[9:]
        left_buf, right_buf, left_sem, right_sem, sum_ref, start_ref, slope_ref, tail_sem = refs
        early = [
            pltpu.make_async_copy(start_hbm, start_ref, tail_sem.at[0]),
            pltpu.make_async_copy(slope_hbm, slope_ref, tail_sem.at[1]),
        ]
    else:
        sum_ref, left_buf, right_buf, left_sem, right_sem = refs
    half = sum_ref.shape[1] // 2

    def copies(n):
        slot = n % SLOTS
        one = pltpu.make_async_copy(pieces[n], left_buf.at[slot], left_sem.at[slot])
        one.start()
        waits = [one]
        place = index_ref[n]
        for part in range(2):
            rows = pl.ds(part * half, half)
            target = right_buf.at[slot, rows]
            sem = right_sem.at[slot, part]
            for which, source in enumerate(
                (
                    near_own.at[place % 4, rows],
                    near_other.at[place % 4, rows],
                    far_own[part].at[place % 4],
                    far_other[part].at[place % 4],
                )
            ):

                @pl.when(place // 4 == which)
                def _(source=source):
                    pltpu.make_async_copy(source, target, sem).start()

            waits.append(pltpu.make_async_copy(near_own.at[0, rows], target, sem))
        return waits

    ahead = SLOTS - 1
    waits = [copies(n) for n in range(min(ahead, count))]
    for n in range(count):
        if n + ahead < count:
            waits.append(copies(n + ahead))
        elif n + ahead == count:
            for copy in early:
                copy.start()
        for wait in waits[n]:
            wait.wait()
        product = lax.dot_general(
            left_buf[n % SLOTS], right_buf[n % SLOTS], TRANSPOSED, preferred_element_type=F32
        )
        if n:
            sum_ref[...] += product
        else:
            sum_ref[...] = product

    if last:
        column = index_ref[count]
        for copy in early:
            copy.wait()
        pairs = down_ref.shape[0]
        span = left_ref.shape[0] // pairs
        for p in range(pairs):
            here = pl.ds(p * span, span)
            if p % 2 == 0:
                two = pl.ds(p * span, 2 * span)
                total = (sum_ref[two, :] + start_ref[two, :]) * slope_ref[two, :].astype(F32)
                e = jnp.dot(total.astype(BF16), proj_ref[...], preferred_element_type=F32)
                e = e.astype(BF16)
            gates = lax.dot_general(
                left_ref[here, :],
                e[(p % 2) * span : (p % 2 + 1) * span],
                (((0,), (0,)), ((), ())),
                preferred_element_type=F32,
            )
            total = (down_ref[p] + gates).reshape(2, 4, 8, 128)
            for m in range(4):
                for away in range(4):

                    @pl.when((column + away) % 4 == m)
                    def _(m=m, away=away, total=total):
                        out_refs[away][:, p] = total[:, m]


ANYWHERE = pl.BlockSpec(memory_space=pl.ANY)
IN_VMEM = pl.BlockSpec(memory_space=pltpu.VMEM)
IN_SMEM = pl.BlockSpec(memory_space=pltpu.SMEM)


def products(pieces, weights, index, tail=()):
    count = len(pieces)
    rows, depth = pieces[0].shape
    units = weights[0].shape[1]
    last = bool(tail)
    scratch = [
        pltpu.VMEM((SLOTS, rows, depth), BF16),
        pltpu.VMEM((SLOTS, units, depth), BF16),
        pltpu.SemaphoreType.DMA((SLOTS,)),
        pltpu.SemaphoreType.DMA((SLOTS, 2)),
    ]
    out_shape = jax.ShapeDtypeStruct((rows, units), F32)
    out_specs = IN_VMEM
    if last:
        scratch += [
            pltpu.VMEM((rows, units), F32),
            pltpu.VMEM((rows, units), F32),
            pltpu.VMEM((rows, units), BF16),
            pltpu.SemaphoreType.DMA((2,)),
        ]
        out_shape = [jax.ShapeDtypeStruct((2, tail[4].shape[0], 8, 128), F32)] * 4
        out_specs = [IN_VMEM] * 4
    return pl.pallas_call(
        lambda *refs: product_kernel(count, last, *refs),
        out_shape=out_shape,
        in_specs=[IN_SMEM]
        + [ANYWHERE] * (count + len(weights) + min(len(tail), 2))
        + [IN_VMEM] * max(len(tail) - 2, 0),
        out_specs=out_specs,
        scratch_shapes=scratch,
        compiler_params=pltpu.CompilerParams(vmem_limit_bytes=58 * 2**20),
        cost_estimate=pl.CostEstimate(
            flops=2 * count * rows * units * depth,
            bytes_accessed=2 * count * (rows + units) * depth + 4 * rows * units,
            transcendentals=0,
        ),
    )(index, *pieces, *weights, *tail)


def sum_columns(slabs):
    total = slabs[0]
    for step in (1, 2, 3):
        total = total + move(slabs[step], shift_x(step))
    return total


def gather_pairs(value, zh, y, c):
    halves = jnp.zeros((2,) + value.shape, value.dtype)
    halves = put(halves, value, zh)
    halves = put(halves, move(value, swap_half), 1 - zh)
    rows = jnp.zeros((4,) + halves.shape, value.dtype)
    rows = put(rows, halves, y)
    for step in (1, 2, 3):
        rows = put(rows, move(halves, shift_y(step)), (y - step) % 4)
    every = jnp.zeros((2,) + rows.shape, value.dtype)
    every = put(every, rows, c)
    every = put(every, move(rows, swap_core), 1 - c)
    return every


def local(
    layer_input,
    gate_saved,
    up_saved,
    grad_out,
    down_weight,
    hidden_proj,
    model_proj,
    query_sketch,
    resp_lengths,
    chosen_index,
):
    tok_rows = grad_out.shape[0]
    pairs = resp_lengths.shape[0]
    span = tok_rows // pairs
    half = span // 2
    sk = hidden_proj.shape[1]
    entries = 2 * sk * sk
    i = lax.axis_index("dp")
    j = lax.axis_index("tensor")
    zh, y, c = i // 8, (i // 2) % 4, i % 2
    zl, x = j // 4, j % 4
    sign = 1 - 2 * c

    def turn(*values):
        return lax.optimization_barrier(values)

    def along_y(value):
        groups = [[(h * 4 + r) * 2 + k for r in range(4)] for h in range(2) for k in range(2)]
        return lax.all_gather(value, "dp", axis=0, tiled=False, axis_index_groups=groups)

    sixteenth = tok_rows // 16
    mid = down_weight.shape[0] // 2
    near_own = along_y(down_weight)

    terms = jnp.concatenate(
        [
            jnp.dot(grad_out, model_proj, preferred_element_type=F32),
            jnp.dot(layer_input, model_proj, preferred_element_type=F32),
        ],
        axis=1,
    ).astype(BF16)
    dealt = lax.all_to_all(terms, "tensor", 0, 0, tiled=True)
    hop1 = move(grad_out, line_z_both)
    ahead0 = move(grad_out, ring_x(1))
    behind0 = move(grad_out, ring_x(-1))
    across0 = move(grad_out, shift_x(2))
    far_a = move(down_weight[:mid], swap_half)
    hop1, ahead0, behind0, across0, far_a, weight_rows, dealt, near_own = turn(
        hop1, ahead0, behind0, across0, far_a, down_weight, dealt, near_own
    )

    far_own_a = along_y(far_a)
    mine = dealt.reshape(16, sixteenth, 2 * sk).astype(F32).sum(axis=0).astype(BF16)
    full = lax.all_to_all(
        jnp.broadcast_to(mine, (16, sixteenth, 2 * sk)).reshape(tok_rows, 2 * sk),
        "tensor", 0, 0, tiled=True,
    )
    hop2 = move(hop1, line_z_both)
    ahead1 = move(hop1, ring_x(1))
    behind1 = move(hop1, ring_x(-1))
    across1 = move(hop1, shift_x(2))
    far_b = move(weight_rows[mid:], swap_half)
    hop2, ahead1, behind1, across1, far_b, far_own_a, full, near_own, gate_saved = turn(
        hop2, ahead1, behind1, across1, far_b, far_own_a, full, near_own, gate_saved
    )

    far_own_b = along_y(far_b)
    gate32 = gate_saved.astype(F32)
    up32 = up_saved.astype(F32)
    sig = jax.nn.sigmoid(gate32)
    hidden = (gate32 * sig * up32).astype(BF16)
    slope = (up32 * sig * (1.0 + gate32 * (1.0 - sig))).astype(BF16)
    a = jnp.dot(hidden, hidden_proj, preferred_element_type=F32)
    hop3 = move(hop2, line_z_both)
    ahead2 = move(hop2, ring_x(1))
    behind2 = move(hop2, ring_x(-1))
    across2 = move(jnp.where(c == 0, hop2, across1), across_both)
    near_other = move(near_own, swap_core)
    hop3, ahead2, behind2, across2, near_other, far_own_a, far_own_b, slope, a = turn(
        hop3, ahead2, behind2, across2, near_other, far_own_a, far_own_b, slope, a
    )
    full = full.astype(F32)

    ahead3 = move(hop3, ring_x(1))
    behind3 = move(hop3, ring_x(-1))
    across3 = move(across2, line_z_both)
    far_other_a = move(far_own_a, swap_core)
    far_other_b = move(far_own_b, swap_core)
    pieces = [
        grad_out, ahead0, behind0, across0,
        hop1, ahead1, behind1, across1,
        hop2, ahead2, behind2, across2,
        hop3, ahead3, behind3, across3,
    ]
    k = jnp.stack(
        [
            ((zl - hop * sign) % 4) * 4 + (x + away) % 4
            for hop in range(4)
            for away in (0, -sign, sign, 2)
        ]
    ).astype(jnp.int32)
    index = jnp.where(k // 8 == zh, 0, 8) + jnp.where(k % 2 == c, 0, 4) + (k // 2) % 4

    slots = jnp.arange(half, dtype=jnp.int32)
    sides = jnp.arange(2, dtype=jnp.int32)
    live = slots[None, None, :] < resp_lengths[:, :, None]
    signs = jnp.where(sides[None, :] == chosen_index[:, None], SCALE, -SCALE).astype(F32)
    weight = jnp.where(live, signs[:, :, None], 0.0).reshape(tok_rows, 1)

    down = jnp.einsum(
        "ptk,ptl->pkl",
        (a * weight).reshape(pairs, span, sk),
        full[:, :sk].reshape(pairs, span, sk),
        precision=lax.Precision.HIGH,
    )
    down = jnp.pad(down, ((0, 0), (0, 0), (0, sk)))
    left = (full[:, sk:] * weight).astype(BF16)
    proj = jnp.pad(hidden_proj, ((0, 0), (sk, 0)))

    weights = (near_own, near_other, far_own_a, far_own_b, far_other_a, far_other_b)
    first = products(pieces[:12], weights, index[:12])
    slabs = products(
        pieces[12:],
        weights,
        jnp.concatenate([index[12:], x.astype(jnp.int32)[None]]),
        (first, slope, proj, left, down),
    )

    both = sum_columns(slabs)
    line = zl % 2
    out = pick(both, line, 0)
    for step in (1, 2, 3):
        out = out + move(pick(both, (line + step) % 2, 0), line_z(step))
    mine = jnp.where(zl >= 2, out[:, :, sk:], out[:, :, :sk])
    sketch = mine.reshape(pairs, 8 * sk)
    every = gather_pairs(sketch, zh, y, c)
    partial = lax.dot_general(
        every.reshape(16 * pairs, 8 * sk),
        query_sketch.astype(F32),
        TRANSPOSED,
        precision=lax.Precision.HIGHEST,
        preferred_element_type=F32,
    ) / jnp.sqrt(F32(entries))
    partial = partial.reshape(2, 2, 2, 2, pairs, -1).transpose(2, 0, 3, 1, 4, 5)
    grid = partial.reshape(4, 4, pairs, -1)
    summed = sum_columns([pick(grid, (x + step) % 4, 0) for step in range(4)])
    scores = pick(summed, zl, 0)
    for step in (1, 2, 3):
        scores = scores + move(pick(summed, (zl + step) % 4, 0), line_z(step))
    return (sketch, scores)


def solution(mesh):
    return jax.shard_map(
        local,
        mesh=mesh,
        in_specs=(
            P("dp", "tensor"),
            P("dp", "tensor"),
            P("dp", "tensor"),
            P("dp", "tensor"),
            P("tensor", "dp"),
            P("tensor", None),
            P("tensor", None),
            P("dp", "tensor"),
            P("dp", None),
            P("dp"),
        ),
        out_specs=(P("dp", "tensor"), P("tensor", "dp")),
        check_vma=False,
    )
```

```python
import jax
import jax.numpy as jnp
from jax import lax
from jax.experimental import pallas as pl
from jax.experimental.pallas import tpu as pltpu
from jax.sharding import PartitionSpec as P

SCALE = 0.25
AXES = ("dp", "tensor")
F32 = jnp.float32
BF16 = jnp.bfloat16
TRANSPOSED = (((1,), (1,)), ((), ()))


def flat(x, y, z, c):
    return (((z // 4) * 4 + y) * 2 + c) * 16 + (z % 4) * 4 + x


def move(value, where):
    pairs = []
    for z in range(8):
        for y in range(4):
            for x in range(4):
                for c in range(2):
                    nx, ny, nz, nc = where(x, y, z, c)
                    pairs.append((flat(x, y, z, c), flat(nx % 4, ny % 4, nz % 8, nc % 2)))
    return lax.ppermute(value, AXES, pairs)


def side(c):
    return 1 - 2 * c


def ring_x(sign):
    return lambda x, y, z, c: (x + sign * side(c), y, z, c)


def ring_y(sign):
    return lambda x, y, z, c: (x, y + sign * side(c), z, c)


def shift_x(step):
    return lambda x, y, z, c: (x + step, y, z, c)


def shift_y(step):
    return lambda x, y, z, c: (x, y + step, z, c)


def line_z(step):
    return lambda x, y, z, c: (x, y, (z // 4) * 4 + (z + step) % 4, c)


def line_z_both(x, y, z, c):
    return line_z(side(c))(x, y, z, c)


def across_both(x, y, z, c):
    return shift_x(2)(x, y, z, c) if c == 0 else line_z_both(x, y, z, c)


def swap_core(x, y, z, c):
    return (x, y, z, c + 1)


def swap_half(x, y, z, c):
    return (x, y, z + 4, c)


def pick(buffer, index, axis):
    return lax.dynamic_index_in_dim(buffer, index, axis, keepdims=False)


def put(buffer, value, index):
    return lax.dynamic_update_index_in_dim(buffer, value, index, 0)


SLOTS = 4


def product_kernel(count, last, index_ref, *refs):
    pieces, refs = refs[:count], refs[count:]
    near_own, near_other, far_own, far_other, refs = refs[0], refs[1], refs[2:4], refs[4:6], refs[6:]
    early = []
    if last:
        start_hbm, slope_hbm, proj_ref, left_ref, down_ref = refs[:5]
        out_refs, refs = refs[5:9], refs[9:]
        left_buf, right_buf, left_sem, right_sem, sum_ref, start_ref, slope_ref, tail_sem = refs[:8]
        sketch_ref = refs[8]
        early = [
            pltpu.make_async_copy(start_hbm, start_ref, tail_sem.at[0]),
            pltpu.make_async_copy(slope_hbm, slope_ref, tail_sem.at[1]),
        ]
    else:
        sum_ref, left_buf, right_buf, left_sem, right_sem = refs
    half = sum_ref.shape[1] // 2

    def copies(n):
        slot = n % SLOTS
        one = pltpu.make_async_copy(pieces[n], left_buf.at[slot], left_sem.at[slot])
        one.start()
        waits = [one]
        place = index_ref[n]
        for part in range(2):
            rows = pl.ds(part * half, half)
            target = right_buf.at[slot, rows]
            sem = right_sem.at[slot, part]
            for which, source in enumerate(
                (
                    near_own.at[place % 4, rows],
                    near_other.at[place % 4, rows],
                    far_own[part].at[place % 4],
                    far_other[part].at[place % 4],
                )
            ):

                @pl.when(place // 4 == which)
                def _(source=source):
                    pltpu.make_async_copy(source, target, sem).start()

            waits.append(pltpu.make_async_copy(near_own.at[0, rows], target, sem))
        return waits

    ahead = SLOTS - 1
    waits = [copies(n) for n in range(min(ahead, count))]
    for n in range(count):
        if n + ahead < count:
            waits.append(copies(n + ahead))
        elif n + ahead == count:
            for copy in early:
                copy.start()
        for wait in waits[n]:
            wait.wait()
        product = lax.dot_general(
            left_buf[n % SLOTS], right_buf[n % SLOTS], TRANSPOSED, preferred_element_type=F32
        )
        if n:
            sum_ref[...] += product
        else:
            sum_ref[...] = product

    if last:
        column = index_ref[count]
        for copy in early:
            copy.wait()
        pairs = down_ref.shape[0]
        span = left_ref.shape[0] // pairs
        for p in range(pairs):
            here = pl.ds(p * span, span)
            if p % 2 == 0:
                two = pl.ds(p * span, 2 * span)
                total = (sum_ref[two, :] + start_ref[two, :]) * slope_ref[two, :].astype(F32)
                e = jnp.dot(total.astype(BF16), proj_ref[...], preferred_element_type=F32)
                e = e.astype(BF16)
            gates = lax.dot_general(
                left_ref[here, :],
                e[(p % 2) * span : (p % 2 + 1) * span],
                (((0,), (0,)), ((), ())),
                preferred_element_type=F32,
            )
            sketch_ref[:, p] = (down_ref[p] + gates).reshape(8, 8, 128)
        for first in range(4):

            @pl.when(column == first)
            def _(first=first):
                for away in range(4):
                    here = (first + away) % 4
                    out_refs[away][0] = sketch_ref[here]
                    out_refs[away][1] = sketch_ref[4 + here]


ANYWHERE = pl.BlockSpec(memory_space=pl.ANY)
IN_VMEM = pl.BlockSpec(memory_space=pltpu.VMEM)
IN_SMEM = pl.BlockSpec(memory_space=pltpu.SMEM)


def products(pieces, weights, index, tail=()):
    count = len(pieces)
    rows, depth = pieces[0].shape
    units = weights[0].shape[1]
    last = bool(tail)
    scratch = [
        pltpu.VMEM((SLOTS, rows, depth), BF16),
        pltpu.VMEM((SLOTS, units, depth), BF16),
        pltpu.SemaphoreType.DMA((SLOTS,)),
        pltpu.SemaphoreType.DMA((SLOTS, 2)),
    ]
    out_shape = jax.ShapeDtypeStruct((rows, units), F32)
    out_specs = IN_VMEM
    if last:
        scratch += [
            pltpu.VMEM((rows, units), F32),
            pltpu.VMEM((rows, units), F32),
            pltpu.VMEM((rows, units), BF16),
            pltpu.SemaphoreType.DMA((2,)),
            pltpu.VMEM((8, tail[4].shape[0], 8, 128), F32),
        ]
        out_shape = [jax.ShapeDtypeStruct((2, tail[4].shape[0], 8, 128), F32)] * 4
        out_specs = [IN_VMEM] * 4
    return pl.pallas_call(
        lambda *refs: product_kernel(count, last, *refs),
        out_shape=out_shape,
        in_specs=[IN_SMEM]
        + [ANYWHERE] * (count + len(weights) + min(len(tail), 2))
        + [IN_VMEM] * max(len(tail) - 2, 0),
        out_specs=out_specs,
        scratch_shapes=scratch,
        compiler_params=pltpu.CompilerParams(vmem_limit_bytes=58 * 2**20),
        cost_estimate=pl.CostEstimate(
            flops=2 * count * rows * units * depth,
            bytes_accessed=2 * count * (rows + units) * depth + 4 * rows * units,
            transcendentals=0,
        ),
    )(index, *pieces, *weights, *tail)


def sum_columns(slabs):
    total = slabs[0]
    for step in (1, 2, 3):
        total = total + move(slabs[step], shift_x(step))
    return total


def gather_pairs(value, zh, y, c):
    halves = jnp.zeros((2,) + value.shape, value.dtype)
    halves = put(halves, value, zh)
    halves = put(halves, move(value, swap_half), 1 - zh)
    rows = jnp.zeros((4,) + halves.shape, value.dtype)
    rows = put(rows, halves, y)
    for step in (1, 2, 3):
        rows = put(rows, move(halves, shift_y(step)), (y - step) % 4)
    every = jnp.zeros((2,) + rows.shape, value.dtype)
    every = put(every, rows, c)
    every = put(every, move(rows, swap_core), 1 - c)
    return every


def local(
    layer_input,
    gate_saved,
    up_saved,
    grad_out,
    down_weight,
    hidden_proj,
    model_proj,
    query_sketch,
    resp_lengths,
    chosen_index,
):
    tok_rows = grad_out.shape[0]
    pairs = resp_lengths.shape[0]
    span = tok_rows // pairs
    half = span // 2
    sk = hidden_proj.shape[1]
    entries = 2 * sk * sk
    i = lax.axis_index("dp")
    j = lax.axis_index("tensor")
    zh, y, c = i // 8, (i // 2) % 4, i % 2
    zl, x = j // 4, j % 4
    sign = 1 - 2 * c

    def turn(*values):
        return lax.optimization_barrier(values)

    def along_y(value):
        groups = [[(h * 4 + r) * 2 + k for r in range(4)] for h in range(2) for k in range(2)]
        return lax.all_gather(value, "dp", axis=0, tiled=False, axis_index_groups=groups)

    sixteenth = tok_rows // 16
    mid = down_weight.shape[0] // 2
    near_own = along_y(down_weight)

    terms = jnp.concatenate(
        [
            jnp.dot(grad_out, model_proj, preferred_element_type=F32),
            jnp.dot(layer_input, model_proj, preferred_element_type=F32),
        ],
        axis=1,
    ).astype(BF16)
    dealt = lax.all_to_all(terms, "tensor", 0, 0, tiled=True)
    hop1 = move(grad_out, line_z_both)
    ahead0 = move(grad_out, ring_x(1))
    behind0 = move(grad_out, ring_x(-1))
    across0 = move(grad_out, shift_x(2))
    far_a = move(down_weight[:mid], swap_half)
    hop1, ahead0, behind0, across0, far_a, weight_rows, dealt, near_own = turn(
        hop1, ahead0, behind0, across0, far_a, down_weight, dealt, near_own
    )

    far_own_a = along_y(far_a)
    mine = dealt.reshape(16, sixteenth, 2 * sk).astype(F32).sum(axis=0).astype(BF16)
    full = lax.all_to_all(
        jnp.broadcast_to(mine, (16, sixteenth, 2 * sk)).reshape(tok_rows, 2 * sk),
        "tensor", 0, 0, tiled=True,
    )
    hop2 = move(hop1, line_z_both)
    ahead1 = move(hop1, ring_x(1))
    behind1 = move(hop1, ring_x(-1))
    across1 = move(hop1, shift_x(2))
    far_b = move(weight_rows[mid:], swap_half)
    hop2, ahead1, behind1, across1, far_b, far_own_a, full, near_own, gate_saved = turn(
        hop2, ahead1, behind1, across1, far_b, far_own_a, full, near_own, gate_saved
    )

    far_own_b = along_y(far_b)
    gate32 = gate_saved.astype(F32)
    up32 = up_saved.astype(F32)
    sig = jax.nn.sigmoid(gate32)
    hidden = (gate32 * sig * up32).astype(BF16)
    slope = (up32 * sig * (1.0 + gate32 * (1.0 - sig))).astype(BF16)
    a = jnp.dot(hidden, hidden_proj, preferred_element_type=F32)
    full = full.astype(F32)

    slots = jnp.arange(half, dtype=jnp.int32)
    sides = jnp.arange(2, dtype=jnp.int32)
    live = slots[None, None, :] < resp_lengths[:, :, None]
    signs = jnp.where(sides[None, :] == chosen_index[:, None], SCALE, -SCALE).astype(F32)
    weight = jnp.where(live, signs[:, :, None], 0.0).reshape(tok_rows, 1)

    down = jnp.einsum(
        "ptk,ptl->pkl",
        (a * weight).reshape(pairs, span, sk),
        full[:, :sk].reshape(pairs, span, sk),
        precision=lax.Precision.HIGH,
    )
    down = jnp.pad(down, ((0, 0), (0, 0), (0, sk)))
    left = (full[:, sk:] * weight).astype(BF16)
    proj = jnp.pad(hidden_proj, ((0, 0), (sk, 0)))

    hop3 = move(hop2, line_z_both)
    ahead2 = move(hop2, ring_x(1))
    behind2 = move(hop2, ring_x(-1))
    across2 = move(jnp.where(c == 0, hop2, across1), across_both)
    near_other = move(near_own, swap_core)
    hop3, ahead2, behind2, across2, near_other, far_own_a, far_own_b, slope, left, down, proj = turn(
        hop3, ahead2, behind2, across2, near_other, far_own_a, far_own_b, slope, left, down, proj
    )
    ahead3 = move(hop3, ring_x(1))
    behind3 = move(hop3, ring_x(-1))
    across3 = move(across2, line_z_both)
    far_other_a = move(far_own_a, swap_core)
    far_other_b = move(far_own_b, swap_core)
    pieces = [
        grad_out, ahead0, behind0, across0,
        hop1, ahead1, behind1, across1,
        hop2, ahead2, behind2, across2,
        hop3, ahead3, behind3, across3,
    ]
    k = jnp.stack(
        [
            ((zl - hop * sign) % 4) * 4 + (x + away) % 4
            for hop in range(4)
            for away in (0, -sign, sign, 2)
        ]
    ).astype(jnp.int32)
    index = jnp.where(k // 8 == zh, 0, 8) + jnp.where(k % 2 == c, 0, 4) + (k // 2) % 4

    weights = (near_own, near_other, far_own_a, far_own_b, far_other_a, far_other_b)
    first = products(pieces[:12], weights, index[:12])
    slabs = products(
        pieces[12:],
        weights,
        jnp.concatenate([index[12:], x.astype(jnp.int32)[None]]),
        (first, slope, proj, left, down),
    )

    both = sum_columns(slabs)
    line = zl % 2
    out = pick(both, line, 0)
    for step in (1, 2, 3):
        out = out + move(pick(both, (line + step) % 2, 0), line_z(step))
    mine = jnp.where(zl >= 2, out[:, :, sk:], out[:, :, :sk])
    sketch = mine.reshape(pairs, 8 * sk)
    every = gather_pairs(sketch, zh, y, c)
    partial = lax.dot_general(
        every.reshape(16 * pairs, 8 * sk),
        query_sketch.astype(F32),
        TRANSPOSED,
        precision=lax.Precision.HIGHEST,
        preferred_element_type=F32,
    ) / jnp.sqrt(F32(entries))
    partial = partial.reshape(2, 2, 2, 2, pairs, -1).transpose(2, 0, 3, 1, 4, 5)
    grid = partial.reshape(4, 4, pairs, -1)
    summed = sum_columns([pick(grid, (x + step) % 4, 0) for step in range(4)])
    scores = pick(summed, zl, 0)
    for step in (1, 2, 3):
        scores = scores + move(pick(summed, (zl + step) % 4, 0), line_z(step))
    return (sketch, scores)


def solution(mesh):
    return jax.shard_map(
        local,
        mesh=mesh,
        in_specs=(
            P("dp", "tensor"),
            P("dp", "tensor"),
            P("dp", "tensor"),
            P("dp", "tensor"),
            P("tensor", "dp"),
            P("tensor", None),
            P("tensor", None),
            P("dp", "tensor"),
            P("dp", None),
            P("dp"),
        ),
        out_specs=(P("dp", "tensor"), P("tensor", "dp")),
        check_vma=False,
    )
```

```python
import jax
import jax.numpy as jnp
from jax import lax
from jax.experimental import pallas as pl
from jax.experimental.pallas import tpu as pltpu
from jax.sharding import PartitionSpec as P

SCALE = 0.25
AXES = ("dp", "tensor")
F32 = jnp.float32
BF16 = jnp.bfloat16
TRANSPOSED = (((1,), (1,)), ((), ()))


def flat(x, y, z, c):
    return (((z // 4) * 4 + y) * 2 + c) * 16 + (z % 4) * 4 + x


def move(value, where):
    pairs = []
    for z in range(8):
        for y in range(4):
            for x in range(4):
                for c in range(2):
                    nx, ny, nz, nc = where(x, y, z, c)
                    pairs.append((flat(x, y, z, c), flat(nx % 4, ny % 4, nz % 8, nc % 2)))
    return lax.ppermute(value, AXES, pairs)


def side(c):
    return 1 - 2 * c


def ring_x(sign):
    return lambda x, y, z, c: (x + sign * side(c), y, z, c)


def ring_y(sign):
    return lambda x, y, z, c: (x, y + sign * side(c), z, c)


def shift_x(step):
    return lambda x, y, z, c: (x + step, y, z, c)


def shift_y(step):
    return lambda x, y, z, c: (x, y + step, z, c)


def line_z(step):
    return lambda x, y, z, c: (x, y, (z // 4) * 4 + (z + step) % 4, c)


def line_z_both(x, y, z, c):
    return line_z(side(c))(x, y, z, c)


def across_both(x, y, z, c):
    return shift_x(2)(x, y, z, c) if c == 0 else line_z_both(x, y, z, c)


def swap_core(x, y, z, c):
    return (x, y, z, c + 1)


def swap_half(x, y, z, c):
    return (x, y, z + 4, c)


def pick(buffer, index, axis):
    return lax.dynamic_index_in_dim(buffer, index, axis, keepdims=False)


def put(buffer, value, index):
    return lax.dynamic_update_index_in_dim(buffer, value, index, 0)


SLOTS = 4


def product_kernel(count, last, index_ref, *refs):
    pieces, refs = refs[:count], refs[count:]
    near_own, near_other, far_own, far_other, refs = refs[0], refs[1], refs[2:4], refs[4:6], refs[6:]
    early = []
    if last:
        start_hbm, slope_hbm, proj_ref, left_ref, down_ref = refs[:5]
        out_refs, refs = refs[5:9], refs[9:]
        left_buf, right_buf, left_sem, right_sem, sum_ref, start_ref, slope_ref, tail_sem = refs[:8]
        sketch_ref = refs[8]
        early = [
            pltpu.make_async_copy(start_hbm, start_ref, tail_sem.at[0]),
            pltpu.make_async_copy(slope_hbm, slope_ref, tail_sem.at[1]),
        ]
    else:
        sum_ref, left_buf, right_buf, left_sem, right_sem = refs
    half = sum_ref.shape[1] // 2

    def copies(n):
        slot = n % SLOTS
        one = pltpu.make_async_copy(pieces[n], left_buf.at[slot], left_sem.at[slot])
        one.start()
        waits = [one]
        place = index_ref[n]
        for part in range(2):
            rows = pl.ds(part * half, half)
            target = right_buf.at[slot, rows]
            sem = right_sem.at[slot, part]
            for which, source in enumerate(
                (
                    near_own.at[place % 4, rows],
                    near_other.at[place % 4, rows],
                    far_own[part].at[place % 4],
                    far_other[part].at[place % 4],
                )
            ):

                @pl.when(place // 4 == which)
                def _(source=source):
                    pltpu.make_async_copy(source, target, sem).start()

            waits.append(pltpu.make_async_copy(near_own.at[0, rows], target, sem))
        return waits

    ahead = SLOTS - 1
    waits = [copies(n) for n in range(min(ahead, count))]
    for n in range(count):
        if n + ahead < count:
            waits.append(copies(n + ahead))
        elif n + ahead == count:
            for copy in early:
                copy.start()
        for wait in waits[n]:
            wait.wait()
        product = lax.dot_general(
            left_buf[n % SLOTS], right_buf[n % SLOTS], TRANSPOSED, preferred_element_type=F32
        )
        if n:
            sum_ref[...] += product
        else:
            sum_ref[...] = product

    if last:
        column = index_ref[count]
        for copy in early:
            copy.wait()
        pairs = down_ref.shape[0]
        span = left_ref.shape[0] // pairs
        for p in range(pairs):
            here = pl.ds(p * span, span)
            if p % 2 == 0:
                two = pl.ds(p * span, 2 * span)
                total = (sum_ref[two, :] + start_ref[two, :]) * slope_ref[two, :].astype(F32)
                e = jnp.dot(total.astype(BF16), proj_ref[...], preferred_element_type=F32)
                e_high = e.astype(BF16)
                e_low = (e - e_high.astype(F32)).astype(BF16)
            gates = None
            for e_part in (e_high, e_low):
                product = lax.dot_general(
                    left_ref[here, :],
                    e_part[(p % 2) * span : (p % 2 + 1) * span],
                    (((0,), (0,)), ((), ())),
                    preferred_element_type=F32,
                )
                gates = product if gates is None else gates + product
            sketch_ref[:, p] = (down_ref[p] + gates).reshape(8, 8, 128)
        for first in range(4):

            @pl.when(column == first)
            def _(first=first):
                for away in range(4):
                    here = (first + away) % 4
                    out_refs[away][0] = sketch_ref[here]
                    out_refs[away][1] = sketch_ref[4 + here]


ANYWHERE = pl.BlockSpec(memory_space=pl.ANY)
IN_VMEM = pl.BlockSpec(memory_space=pltpu.VMEM)
IN_SMEM = pl.BlockSpec(memory_space=pltpu.SMEM)


def products(pieces, weights, index, tail=()):
    count = len(pieces)
    rows, depth = pieces[0].shape
    units = weights[0].shape[1]
    last = bool(tail)
    scratch = [
        pltpu.VMEM((SLOTS, rows, depth), BF16),
        pltpu.VMEM((SLOTS, units, depth), BF16),
        pltpu.SemaphoreType.DMA((SLOTS,)),
        pltpu.SemaphoreType.DMA((SLOTS, 2)),
    ]
    out_shape = jax.ShapeDtypeStruct((rows, units), F32)
    out_specs = IN_VMEM
    if last:
        scratch += [
            pltpu.VMEM((rows, units), F32),
            pltpu.VMEM((rows, units), F32),
            pltpu.VMEM((rows, units), BF16),
            pltpu.SemaphoreType.DMA((2,)),
            pltpu.VMEM((8, tail[4].shape[0], 8, 128), F32),
        ]
        out_shape = [jax.ShapeDtypeStruct((2, tail[4].shape[0], 8, 128), F32)] * 4
        out_specs = [IN_VMEM] * 4
    return pl.pallas_call(
        lambda *refs: product_kernel(count, last, *refs),
        out_shape=out_shape,
        in_specs=[IN_SMEM]
        + [ANYWHERE] * (count + len(weights) + min(len(tail), 2))
        + [IN_VMEM] * max(len(tail) - 2, 0),
        out_specs=out_specs,
        scratch_shapes=scratch,
        compiler_params=pltpu.CompilerParams(vmem_limit_bytes=58 * 2**20),
        cost_estimate=pl.CostEstimate(
            flops=2 * count * rows * units * depth,
            bytes_accessed=2 * count * (rows + units) * depth + 4 * rows * units,
            transcendentals=0,
        ),
    )(index, *pieces, *weights, *tail)


def sum_columns(slabs):
    total = slabs[0]
    for step in (1, 2, 3):
        total = total + move(slabs[step], shift_x(step))
    return total


def gather_pairs(value, zh, y, c):
    halves = jnp.zeros((2,) + value.shape, value.dtype)
    halves = put(halves, value, zh)
    halves = put(halves, move(value, swap_half), 1 - zh)
    rows = jnp.zeros((4,) + halves.shape, value.dtype)
    rows = put(rows, halves, y)
    for step in (1, 2, 3):
        rows = put(rows, move(halves, shift_y(step)), (y - step) % 4)
    every = jnp.zeros((2,) + rows.shape, value.dtype)
    every = put(every, rows, c)
    every = put(every, move(rows, swap_core), 1 - c)
    return every


def local(
    layer_input,
    gate_saved,
    up_saved,
    grad_out,
    down_weight,
    hidden_proj,
    model_proj,
    query_sketch,
    resp_lengths,
    chosen_index,
):
    tok_rows = grad_out.shape[0]
    pairs = resp_lengths.shape[0]
    span = tok_rows // pairs
    half = span // 2
    sk = hidden_proj.shape[1]
    entries = 2 * sk * sk
    i = lax.axis_index("dp")
    j = lax.axis_index("tensor")
    zh, y, c = i // 8, (i // 2) % 4, i % 2
    zl, x = j // 4, j % 4
    sign = 1 - 2 * c

    def turn(*values):
        return lax.optimization_barrier(values)

    def along_y(value):
        groups = [[(h * 4 + r) * 2 + k for r in range(4)] for h in range(2) for k in range(2)]
        return lax.all_gather(value, "dp", axis=0, tiled=False, axis_index_groups=groups)

    sixteenth = tok_rows // 16
    mid = down_weight.shape[0] // 2
    near_own = along_y(down_weight)

    proj = jnp.pad(hidden_proj, ((0, 0), (sk, 0)))
    terms = jnp.concatenate(
        [
            jnp.dot(grad_out, model_proj, preferred_element_type=F32),
            jnp.dot(layer_input, model_proj, preferred_element_type=F32),
        ],
        axis=1,
    ).astype(BF16)
    dealt = lax.all_to_all(terms, "tensor", 0, 0, tiled=True)
    hop1 = move(grad_out, line_z_both)
    ahead0 = move(grad_out, ring_x(1))
    behind0 = move(grad_out, ring_x(-1))
    across0 = move(grad_out, shift_x(2))
    far_a = move(down_weight[:mid], swap_half)
    hop1, ahead0, behind0, across0, far_a, weight_rows, dealt, proj = turn(
        hop1, ahead0, behind0, across0, far_a, down_weight, dealt, proj
    )

    far_a, near_own = turn(far_a, near_own)
    far_own_a = along_y(far_a)
    mine = dealt.reshape(16, sixteenth, 2 * sk).astype(F32).sum(axis=0).astype(BF16)
    full = lax.all_to_all(
        jnp.broadcast_to(mine, (16, sixteenth, 2 * sk)).reshape(tok_rows, 2 * sk),
        "tensor", 0, 0, tiled=True,
    )
    hop2 = move(hop1, line_z_both)
    ahead1 = move(hop1, ring_x(1))
    behind1 = move(hop1, ring_x(-1))
    across1 = move(hop1, shift_x(2))
    far_b = move(weight_rows[mid:], swap_half)
    hop2, ahead1, behind1, across1, far_b, far_own_a, full, near_own, gate_saved = turn(
        hop2, ahead1, behind1, across1, far_b, far_own_a, full, near_own, gate_saved
    )

    far_own_b = along_y(far_b)
    gate32 = gate_saved.astype(F32)
    up32 = up_saved.astype(F32)
    sig = jax.nn.sigmoid(gate32)
    hidden = (gate32 * sig * up32).astype(BF16)
    slope = (up32 * sig * (1.0 + gate32 * (1.0 - sig))).astype(BF16)
    a = jnp.dot(hidden, hidden_proj, preferred_element_type=F32)
    full = full.astype(F32)

    slots = jnp.arange(half, dtype=jnp.int32)
    sides = jnp.arange(2, dtype=jnp.int32)
    live = slots[None, None, :] < resp_lengths[:, :, None]
    signs = jnp.where(sides[None, :] == chosen_index[:, None], SCALE, -SCALE).astype(F32)
    weight = jnp.where(live, signs[:, :, None], 0.0).reshape(tok_rows, 1)

    down = jnp.einsum(
        "ptk,ptl->pkl",
        (a * weight).reshape(pairs, span, sk),
        full[:, :sk].reshape(pairs, span, sk),
        precision=lax.Precision.HIGH,
    )
    down = jnp.pad(down, ((0, 0), (0, 0), (0, sk)))
    left = (full[:, sk:] * weight).astype(BF16)

    hop3 = move(hop2, line_z_both)
    ahead2 = move(hop2, ring_x(1))
    behind2 = move(hop2, ring_x(-1))
    across2 = move(jnp.where(c == 0, hop2, across1), across_both)
    near_other = move(near_own, swap_core)
    hop3, ahead2, behind2, across2, near_other, far_own_a, far_own_b, slope, left, down = turn(
        hop3, ahead2, behind2, across2, near_other, far_own_a, far_own_b, slope, left, down
    )
    ahead3 = move(hop3, ring_x(1))
    behind3 = move(hop3, ring_x(-1))
    across3 = move(across2, line_z_both)
    far_other_a = move(far_own_a, swap_core)
    far_other_b = move(far_own_b, swap_core)
    pieces = [
        grad_out, ahead0, behind0, across0,
        hop1, ahead1, behind1, across1,
        hop2, ahead2, behind2, across2,
        hop3, ahead3, behind3, across3,
    ]
    k = jnp.stack(
        [
            ((zl - hop * sign) % 4) * 4 + (x + away) % 4
            for hop in range(4)
            for away in (0, -sign, sign, 2)
        ]
    ).astype(jnp.int32)
    index = jnp.where(k // 8 == zh, 0, 8) + jnp.where(k % 2 == c, 0, 4) + (k // 2) % 4

    weights = (near_own, near_other, far_own_a, far_own_b, far_other_a, far_other_b)
    first = products(pieces[:12], weights, index[:12])
    slabs = products(
        pieces[12:],
        weights,
        jnp.concatenate([index[12:], x.astype(jnp.int32)[None]]),
        (first, slope, proj, left, down),
    )

    both = sum_columns(slabs)
    line = zl % 2
    out = pick(both, line, 0)
    for step in (1, 2, 3):
        out = out + move(pick(both, (line + step) % 2, 0), line_z(step))
    mine = jnp.where(zl >= 2, out[:, :, sk:], out[:, :, :sk])
    sketch = mine.reshape(pairs, 8 * sk)
    every = gather_pairs(sketch, zh, y, c)
    partial = lax.dot_general(
        every.reshape(16 * pairs, 8 * sk),
        query_sketch.astype(F32),
        TRANSPOSED,
        precision=lax.Precision.HIGHEST,
        preferred_element_type=F32,
    ) / jnp.sqrt(F32(entries))
    partial = partial.reshape(2, 2, 2, 2, pairs, -1).transpose(2, 0, 3, 1, 4, 5)
    grid = partial.reshape(4, 4, pairs, -1)
    summed = sum_columns([pick(grid, (x + step) % 4, 0) for step in range(4)])
    scores = pick(summed, zl, 0)
    for step in (1, 2, 3):
        scores = scores + move(pick(summed, (zl + step) % 4, 0), line_z(step))
    return (sketch, scores)


def solution(mesh):
    return jax.shard_map(
        local,
        mesh=mesh,
        in_specs=(
            P("dp", "tensor"),
            P("dp", "tensor"),
            P("dp", "tensor"),
            P("dp", "tensor"),
            P("tensor", "dp"),
            P("tensor", None),
            P("tensor", None),
            P("dp", "tensor"),
            P("dp", None),
            P("dp"),
        ),
        out_specs=(P("dp", "tensor"), P("tensor", "dp")),
        check_vma=False,
    )
```

```python
import jax
import jax.numpy as jnp
from jax import lax
from jax.experimental import pallas as pl
from jax.experimental.pallas import tpu as pltpu
from jax.sharding import PartitionSpec as P

SCALE = 0.25
AXES = ("dp", "tensor")
F32 = jnp.float32
BF16 = jnp.bfloat16
TRANSPOSED = (((1,), (1,)), ((), ()))


def flat(x, y, z, c):
    return (((z // 4) * 4 + y) * 2 + c) * 16 + (z % 4) * 4 + x


def move(value, where):
    pairs = []
    for z in range(8):
        for y in range(4):
            for x in range(4):
                for c in range(2):
                    nx, ny, nz, nc = where(x, y, z, c)
                    pairs.append((flat(x, y, z, c), flat(nx % 4, ny % 4, nz % 8, nc % 2)))
    return lax.ppermute(value, AXES, pairs)


def side(c):
    return 1 - 2 * c


def ring_x(sign):
    return lambda x, y, z, c: (x + sign * side(c), y, z, c)


def ring_y(sign):
    return lambda x, y, z, c: (x, y + sign * side(c), z, c)


def shift_x(step):
    return lambda x, y, z, c: (x + step, y, z, c)


def shift_y(step):
    return lambda x, y, z, c: (x, y + step, z, c)


def line_z(step):
    return lambda x, y, z, c: (x, y, (z // 4) * 4 + (z + step) % 4, c)


def line_z_both(x, y, z, c):
    return line_z(side(c))(x, y, z, c)


def across_both(x, y, z, c):
    return shift_x(2)(x, y, z, c) if c == 0 else line_z_both(x, y, z, c)


def swap_core(x, y, z, c):
    return (x, y, z, c + 1)


def swap_half(x, y, z, c):
    return (x, y, z + 4, c)


def pick(buffer, index, axis):
    return lax.dynamic_index_in_dim(buffer, index, axis, keepdims=False)


def put(buffer, value, index):
    return lax.dynamic_update_index_in_dim(buffer, value, index, 0)


SLOTS = 4


def product_kernel(count, last, index_ref, *refs):
    pieces, refs = refs[:count], refs[count:]
    near_own, near_other, far_own, far_other, refs = refs[0], refs[1], refs[2:4], refs[4:6], refs[6:]
    early = []
    if last:
        start_hbm, slope_hbm, proj_ref, left_ref, down_ref = refs[:5]
        out_refs, refs = refs[5:9], refs[9:]
        left_buf, right_buf, left_sem, right_sem, sum_ref, start_ref, slope_ref, tail_sem = refs[:8]
        sketch_ref = refs[8]
        early = [
            pltpu.make_async_copy(start_hbm, start_ref, tail_sem.at[0]),
            pltpu.make_async_copy(slope_hbm, slope_ref, tail_sem.at[1]),
        ]
    else:
        sum_ref, left_buf, right_buf, left_sem, right_sem = refs
    half = sum_ref.shape[1] // 2

    def copies(n):
        slot = n % SLOTS
        one = pltpu.make_async_copy(pieces[n], left_buf.at[slot], left_sem.at[slot])
        one.start()
        waits = [one]
        place = index_ref[n]
        for part in range(2):
            rows = pl.ds(part * half, half)
            target = right_buf.at[slot, rows]
            sem = right_sem.at[slot, part]
            for which, source in enumerate(
                (
                    near_own.at[place % 4, rows],
                    near_other.at[place % 4, rows],
                    far_own[part].at[place % 4],
                    far_other[part].at[place % 4],
                )
            ):

                @pl.when(place // 4 == which)
                def _(source=source):
                    pltpu.make_async_copy(source, target, sem).start()

            waits.append(pltpu.make_async_copy(near_own.at[0, rows], target, sem))
        return waits

    ahead = SLOTS - 1
    waits = [copies(n) for n in range(min(ahead, count))]
    for n in range(count):
        if n + ahead < count:
            waits.append(copies(n + ahead))
        elif n + ahead == count:
            for copy in early:
                copy.start()
        for wait in waits[n]:
            wait.wait()
        product = lax.dot_general(
            left_buf[n % SLOTS], right_buf[n % SLOTS], TRANSPOSED, preferred_element_type=F32
        )
        if n:
            sum_ref[...] += product
        else:
            sum_ref[...] = product

    if last:
        column = index_ref[count]
        for copy in early:
            copy.wait()
        pairs = down_ref.shape[0]
        span = left_ref.shape[0] // pairs
        for p in range(pairs):
            here = pl.ds(p * span, span)
            if p % 2 == 0:
                two = pl.ds(p * span, 2 * span)
                total = (sum_ref[two, :] + start_ref[two, :]) * slope_ref[two, :].astype(F32)
                e = jnp.dot(total.astype(BF16), proj_ref[...], preferred_element_type=F32)
                e_high = e.astype(BF16)
                e_low = (e - e_high.astype(F32)).astype(BF16)
            gates = None
            for e_part in (e_high, e_low):
                product = lax.dot_general(
                    left_ref[here, :],
                    e_part[(p % 2) * span : (p % 2 + 1) * span],
                    (((0,), (0,)), ((), ())),
                    preferred_element_type=F32,
                )
                gates = product if gates is None else gates + product
            sketch_ref[:, p] = (down_ref[p] + gates).reshape(8, 8, 128)
        for first in range(4):

            @pl.when(column == first)
            def _(first=first):
                for away in range(4):
                    here = (first + away) % 4
                    out_refs[away][0] = sketch_ref[here]
                    out_refs[away][1] = sketch_ref[4 + here]


ANYWHERE = pl.BlockSpec(memory_space=pl.ANY)
IN_VMEM = pl.BlockSpec(memory_space=pltpu.VMEM)
IN_SMEM = pl.BlockSpec(memory_space=pltpu.SMEM)


def products(pieces, weights, index, tail=()):
    count = len(pieces)
    rows, depth = pieces[0].shape
    units = weights[0].shape[1]
    last = bool(tail)
    scratch = [
        pltpu.VMEM((SLOTS, rows, depth), BF16),
        pltpu.VMEM((SLOTS, units, depth), BF16),
        pltpu.SemaphoreType.DMA((SLOTS,)),
        pltpu.SemaphoreType.DMA((SLOTS, 2)),
    ]
    out_shape = jax.ShapeDtypeStruct((rows, units), F32)
    out_specs = IN_VMEM
    if last:
        scratch += [
            pltpu.VMEM((rows, units), F32),
            pltpu.VMEM((rows, units), F32),
            pltpu.VMEM((rows, units), BF16),
            pltpu.SemaphoreType.DMA((2,)),
            pltpu.VMEM((8, tail[4].shape[0], 8, 128), F32),
        ]
        out_shape = [jax.ShapeDtypeStruct((2, tail[4].shape[0], 8, 128), F32)] * 4
        out_specs = [IN_VMEM] * 4
    return pl.pallas_call(
        lambda *refs: product_kernel(count, last, *refs),
        out_shape=out_shape,
        in_specs=[IN_SMEM]
        + [ANYWHERE] * (count + len(weights) + min(len(tail), 2))
        + [IN_VMEM] * max(len(tail) - 2, 0),
        out_specs=out_specs,
        scratch_shapes=scratch,
        compiler_params=pltpu.CompilerParams(vmem_limit_bytes=58 * 2**20),
        cost_estimate=pl.CostEstimate(
            flops=2 * count * rows * units * depth,
            bytes_accessed=2 * count * (rows + units) * depth + 4 * rows * units,
            transcendentals=0,
        ),
    )(index, *pieces, *weights, *tail)


def sum_columns(slabs):
    total = slabs[0]
    for step in (1, 2, 3):
        total = total + move(slabs[step], shift_x(step))
    return total


def gather_pairs(value, zh, y, c):
    halves = jnp.zeros((2,) + value.shape, value.dtype)
    halves = put(halves, value, zh)
    halves = put(halves, move(value, swap_half), 1 - zh)
    rows = jnp.zeros((4,) + halves.shape, value.dtype)
    rows = put(rows, halves, y)
    for step in (1, 2, 3):
        rows = put(rows, move(halves, shift_y(step)), (y - step) % 4)
    every = jnp.zeros((2,) + rows.shape, value.dtype)
    every = put(every, rows, c)
    every = put(every, move(rows, swap_core), 1 - c)
    return every


def local(
    layer_input,
    gate_saved,
    up_saved,
    grad_out,
    down_weight,
    hidden_proj,
    model_proj,
    query_sketch,
    resp_lengths,
    chosen_index,
):
    tok_rows = grad_out.shape[0]
    pairs = resp_lengths.shape[0]
    span = tok_rows // pairs
    half = span // 2
    sk = hidden_proj.shape[1]
    entries = 2 * sk * sk
    i = lax.axis_index("dp")
    j = lax.axis_index("tensor")
    zh, y, c = i // 8, (i // 2) % 4, i % 2
    zl, x = j // 4, j % 4
    sign = 1 - 2 * c

    def turn(*values):
        return lax.optimization_barrier(values)

    def along_y(value):
        groups = [[(h * 4 + r) * 2 + k for r in range(4)] for h in range(2) for k in range(2)]
        return lax.all_gather(value, "dp", axis=0, tiled=False, axis_index_groups=groups)

    sixteenth = tok_rows // 16
    mid = down_weight.shape[0] // 2
    near_own = along_y(down_weight)

    proj = jnp.pad(hidden_proj, ((0, 0), (sk, 0)))
    terms = jnp.concatenate(
        [
            jnp.dot(grad_out, model_proj, preferred_element_type=F32),
            jnp.dot(layer_input, model_proj, preferred_element_type=F32),
        ],
        axis=1,
    ).astype(BF16)
    dealt = lax.all_to_all(terms, "tensor", 0, 0, tiled=True)
    hop1 = move(grad_out, line_z_both)
    ahead0 = move(grad_out, ring_x(1))
    behind0 = move(grad_out, ring_x(-1))
    across0 = move(grad_out, shift_x(2))
    far_a = move(down_weight[:mid], swap_half)
    hop1, ahead0, behind0, across0, far_a, weight_rows, dealt, proj = turn(
        hop1, ahead0, behind0, across0, far_a, down_weight, dealt, proj
    )

    far_a, near_own = turn(far_a, near_own)
    far_own_a = along_y(far_a)
    mine = dealt.reshape(16, sixteenth, 2 * sk).astype(F32).sum(axis=0).astype(BF16)
    full = lax.all_to_all(
        jnp.broadcast_to(mine, (16, sixteenth, 2 * sk)).reshape(tok_rows, 2 * sk),
        "tensor", 0, 0, tiled=True,
    )
    hop2 = move(hop1, line_z_both)
    ahead1 = move(hop1, ring_x(1))
    behind1 = move(hop1, ring_x(-1))
    across1 = move(hop1, shift_x(2))
    far_b = move(weight_rows[mid:], swap_half)
    hop2, ahead1, behind1, across1, far_b, far_own_a, full, near_own, gate_saved = turn(
        hop2, ahead1, behind1, across1, far_b, far_own_a, full, near_own, gate_saved
    )

    far_own_b = along_y(far_b)
    gate32 = gate_saved.astype(F32)
    up32 = up_saved.astype(F32)
    sig = jax.nn.sigmoid(gate32)
    hidden = (gate32 * sig * up32).astype(BF16)
    slope = (up32 * sig * (1.0 + gate32 * (1.0 - sig))).astype(BF16)
    a = jnp.dot(hidden, hidden_proj, preferred_element_type=F32)
    full = full.astype(F32)

    slots = jnp.arange(half, dtype=jnp.int32)
    sides = jnp.arange(2, dtype=jnp.int32)
    live = slots[None, None, :] < resp_lengths[:, :, None]
    signs = jnp.where(sides[None, :] == chosen_index[:, None], SCALE, -SCALE).astype(F32)
    weight = jnp.where(live, signs[:, :, None], 0.0).reshape(tok_rows, 1)

    down = jnp.einsum(
        "ptk,ptl->pkl",
        (a * weight).reshape(pairs, span, sk),
        full[:, :sk].reshape(pairs, span, sk),
        precision=lax.Precision.HIGH,
    )
    down = jnp.pad(down, ((0, 0), (0, 0), (0, sk)))
    left = (full[:, sk:] * weight).astype(BF16)

    hop3 = move(hop2, line_z_both)
    ahead2 = move(hop2, ring_x(1))
    behind2 = move(hop2, ring_x(-1))
    across2 = move(jnp.where(c == 0, hop2, across1), across_both)
    near_other = move(near_own, swap_core)
    hop3, across2, ahead2, behind2, near_other, far_own_a, far_own_b, slope, left, down = turn(
        hop3, across2, ahead2, behind2, near_other, far_own_a, far_own_b, slope, left, down
    )
    ahead3 = move(hop3, ring_x(1))
    behind3 = move(hop3, ring_x(-1))
    across3 = move(across2, line_z_both)
    far_other_a = move(far_own_a, swap_core)
    far_other_b = move(far_own_b, swap_core)
    pieces = [
        grad_out, ahead0, behind0, across0,
        hop1, ahead1, behind1, across1,
        hop2, ahead2, behind2, across2,
        hop3, ahead3, behind3, across3,
    ]
    k = jnp.stack(
        [
            ((zl - hop * sign) % 4) * 4 + (x + away) % 4
            for hop in range(4)
            for away in (0, -sign, sign, 2)
        ]
    ).astype(jnp.int32)
    index = jnp.where(k // 8 == zh, 0, 8) + jnp.where(k % 2 == c, 0, 4) + (k // 2) % 4

    weights = (near_own, near_other, far_own_a, far_own_b, far_other_a, far_other_b)
    first = products(pieces[:12], weights, index[:12])
    slabs = products(
        pieces[12:],
        weights,
        jnp.concatenate([index[12:], x.astype(jnp.int32)[None]]),
        (first, slope, proj, left, down),
    )

    both = sum_columns(slabs)
    line = zl % 2
    out = pick(both, line, 0)
    for step in (1, 2, 3):
        out = out + move(pick(both, (line + step) % 2, 0), line_z(step))
    mine = jnp.where(zl >= 2, out[:, :, sk:], out[:, :, :sk])
    sketch = mine.reshape(pairs, 8 * sk)
    every = gather_pairs(sketch, zh, y, c)
    partial = lax.dot_general(
        every.reshape(16 * pairs, 8 * sk),
        query_sketch.astype(F32),
        TRANSPOSED,
        precision=lax.Precision.HIGHEST,
        preferred_element_type=F32,
    ) / jnp.sqrt(F32(entries))
    partial = partial.reshape(2, 2, 2, 2, pairs, -1).transpose(2, 0, 3, 1, 4, 5)
    grid = partial.reshape(4, 4, pairs, -1)
    summed = sum_columns([pick(grid, (x + step) % 4, 0) for step in range(4)])
    scores = pick(summed, zl, 0)
    for step in (1, 2, 3):
        scores = scores + move(pick(summed, (zl + step) % 4, 0), line_z(step))
    return (sketch, scores)


def solution(mesh):
    return jax.shard_map(
        local,
        mesh=mesh,
        in_specs=(
            P("dp", "tensor"),
            P("dp", "tensor"),
            P("dp", "tensor"),
            P("dp", "tensor"),
            P("tensor", "dp"),
            P("tensor", None),
            P("tensor", None),
            P("dp", "tensor"),
            P("dp", None),
            P("dp"),
        ),
        out_specs=(P("dp", "tensor"), P("tensor", "dp")),
        check_vma=False,
    )
```
